512 devices in a mesh: gx: 16 (over z, x_lo), gy: 32 (over y, x_hi, core).
Axes of the slice: x: 4 (x_hi: 2, x_lo: 2; x = x_hi * 2 + x_lo), y: 8, z: 8, core: 2. Of those that a mesh axis runs over, the one named last changes fastest.
Arguments:
- inputs: bfloat16 [1024, 8192], P('gy', 'gx'), may hold values from -6 to 6
- gate_weight: bfloat16 [8192, 16384], P('gx', 'gy'), may hold values from -0.0625 to 0.0625
- up_weight: bfloat16 [8192, 16384], P('gx', 'gy'), may hold values from -0.0625 to 0.0625
- down_weight: bfloat16 [16384, 8192], P('gy', 'gx'), may hold values from -0.046875 to 0.046875
- cotangent: bfloat16 [1024, 8192], P('gy', 'gx'), may hold values from -6 to 6
Outputs:
- input_grad: bfloat16 [1024, 8192], P('gy', 'gx')
- gate_grad: bfloat16 [8192, 16384], P('gx', 'gy')
- up_grad: bfloat16 [8192, 16384], P('gx', 'gy')
- down_grad: bfloat16 [16384, 8192], P('gy', 'gx')
The draws below stay inside these ranges and needn't reach their ends.
All inputs are finite; a program needn't handle non-finite values.
Results may differ from the reference program's by a relative error of at most 0.0049.
Values may be sent and summed in bfloat16 or wider, within the bound.
No kernel may reach another device: no remote copies, remote signals or barrier semaphores. Data moves between devices by JAX's collectives and lax.ppermute only.
A program may use at most 64 MiB of HBM per device.

```python
import jax
import jax.numpy as jnp
from jax import lax

D = 8192
F = 16384
TOKENS = 1024


def block_scale(rng, shape, cuts, smallest, high):
    factor_of, own = 1.0, jax.random.fold_in(rng, 6)
    for axis_at, parts in cuts:
        draws = jnp.exp(jax.random.uniform(jax.random.fold_in(own, axis_at), (parts,), jnp.float32, smallest / len(cuts), high / len(cuts)))
        factor_of = factor_of * jnp.repeat(draws, shape[axis_at] // parts).reshape([-1 if axis == axis_at else 1 for axis in range(len(shape))])
    return factor_of


def gaussian(stream_key, shape, width, bound, pieces=(), dtype=jnp.bfloat16):
    array = jax.random.normal(stream_key, shape, jnp.float32) * width
    if len(pieces) > 0:
        array = block_scale(stream_key, shape, pieces, -0.22, 0.18) * array
    return jnp.clip(array, min=-bound, max=bound).astype(dtype)


def setup_inputs(seed: int = 0) -> dict:
    key_list = jax.random.split(jax.random.key(seed), 6)
    inputs = gaussian(key_list[0], (TOKENS, D), 1.0, 6.0, ((0, 32), (1, 16)))
    gate_weight = gaussian(key_list[1], (D, F), D ** -0.5, 0.0625, ((0, 16), (1, 32)))
    up_weight = gaussian(key_list[2], (D, F), D ** -0.5, 0.0625, ((0, 16), (1, 32)))
    down_weight = gaussian(key_list[3], (F, D), F ** -0.5, 0.046875, ((0, 32), (1, 16)))
    cotangent = gaussian(key_list[4], (TOKENS, D), 1.0, 6.0, ((0, 32), (1, 16)))
    return dict(inputs=inputs, gate_weight=gate_weight, up_weight=up_weight, down_weight=down_weight, cotangent=cotangent)


def reference(inputs, gate_weight, up_weight, down_weight, cotangent):
    gate = jnp.dot(inputs, gate_weight, preferred_element_type=jnp.float32)
    upper = jnp.dot(inputs, up_weight, preferred_element_type=jnp.float32)
    hidden_grad = lax.dot_general(cotangent, down_weight, (((1,), (1,)), ((), ())), preferred_element_type=jnp.float32)
    sig = jax.nn.sigmoid(gate)
    hidden = (gate * sig * upper).astype(jnp.bfloat16)
    gate_delta = (hidden_grad * upper * sig * (1.0 + gate * (1.0 - sig))).astype(jnp.bfloat16)
    up_delta = (hidden_grad * gate * sig).astype(jnp.bfloat16)
    tcon = (((0,), (0,)), ((), ()))
    down_grad = lax.dot_general(hidden, cotangent, tcon, preferred_element_type=jnp.float32).astype(jnp.bfloat16)
    gate_grad = lax.dot_general(inputs, gate_delta, tcon, preferred_element_type=jnp.float32).astype(jnp.bfloat16)
    up_grad = lax.dot_general(inputs, up_delta, tcon, preferred_element_type=jnp.float32).astype(jnp.bfloat16)
    fcon = (((1,), (1,)), ((), ()))
    input_grad = lax.dot_general(gate_delta, gate_weight, fcon, preferred_element_type=jnp.float32)
    input_grad = input_grad + lax.dot_general(up_delta, up_weight, fcon, preferred_element_type=jnp.float32)
    return input_grad.astype(jnp.bfloat16), gate_grad, up_grad, down_grad
```

```python
import jax
import jax.numpy as jnp
from jax import lax
from jax.sharding import Mesh
from jax.sharding import PartitionSpec as P

AXES = ("z", "xl", "y", "xh", "core")
GX, GY = ("z", "xl"), ("y", "xh", "core")
SCALE = 16.0
F32, BF16, F16 = jnp.float32, jnp.bfloat16, jnp.float16


def dot(a, b, ca, cb):
    return lax.dot_general(a, b, (((ca,), (cb,)), ((), ())), preferred_element_type=F32)


def swap(x, axis):
    return lax.ppermute(x, axis, [(0, 1), (1, 0)])


def spread(x, axis, n):
    return lax.all_to_all(jnp.broadcast_to(x[None], (n,) + x.shape), axis, 0, 0, tiled=True)


def per_device(nz, ny, x, wg, wu, wd, c):
    rows, width = x.shape
    fwidth = wg.shape[1]
    z_f = fwidth // nz
    xl, xh, core = lax.axis_index("xl"), lax.axis_index("xh"), lax.axis_index("core")

    pair = jnp.concatenate([x, c], axis=0)
    own = lax.ppermute(pair, ("xl", "xh"), [(0, 0), (3, 2), (1, 1), (2, 3)])
    oth = lax.ppermute(pair, ("xl", "xh"), [(2, 0), (1, 2), (3, 1), (0, 3)])
    wg2, wu2, wd2 = swap(wg, "xl"), swap(wu, "xl"), swap(wd, "xl")
    both = jnp.concatenate([own, oth], axis=1)

    def gather_tokens(t):
        t = spread(t, "y", ny).reshape(ny * rows, 2 * width)
        return lax.all_gather(t, "core", axis=0, tiled=True)

    xs = gather_tokens(both[:rows])
    cs = gather_tokens(both[rows:])
    xo, xt, co, ct = xs[:, :width], xs[:, width:], cs[:, :width], cs[:, width:]
    half = xs.shape[0]

    def sum_over_z(part):
        part = (part * SCALE).astype(F16).reshape(nz, z_f, half)
        return lax.all_to_all(part, "z", 0, 0, tiled=True).astype(F32).sum(0) * (1.0 / SCALE)

    gate = sum_over_z(dot(wg, xo, 0, 1) + dot(wg2, xt, 0, 1))
    upper = sum_over_z(dot(wu, xo, 0, 1) + dot(wu2, xt, 0, 1))
    hidden_grad = sum_over_z(dot(wd, co, 1, 1) + dot(wd2, ct, 1, 1))
    xr, cr = swap(xt, "xl"), swap(ct, "xl")

    sig = jax.nn.sigmoid(gate)
    hidden = (gate * sig * upper).astype(BF16)
    gate_delta = (hidden_grad * upper * sig * (1.0 + gate * (1.0 - sig))).astype(BF16)
    up_delta = (hidden_grad * gate * sig).astype(BF16)

    def gather_hidden(t):
        t = spread(t, "z", nz).reshape(fwidth, half)
        return t, swap(t, "xl")

    gdo, gdr = gather_hidden(gate_delta)
    udo, udr = gather_hidden(up_delta)
    hio, hir = gather_hidden(hidden)

    total_o = dot(gdo, wg, 0, 1) + dot(udo, wu, 0, 1)
    total_r = dot(gdr, wg, 0, 1) + dot(udr, wu, 0, 1)
    total_o = total_o.reshape(2, ny, rows, width)
    total_r = total_r.reshape(2, ny, rows, width)
    same = (xh ^ xl) == 0
    first = core == 0
    halves = jnp.stack([jnp.where(same, total_o, total_r), jnp.where(same, total_r, total_o)], axis=2)
    keep = jnp.where(first, halves[0], halves[1])
    send = jnp.where(first, halves[1], halves[0])
    total = (keep + swap(send, "core")).astype(BF16).reshape(2 * ny, rows, width)
    input_grad = lax.all_to_all(total, ("y", "xh"), 0, 0, tiled=True).astype(F32).sum(0).astype(BF16)

    down_grad = (dot(hio, co, 1, 0) + dot(hir, cr, 1, 0)).astype(BF16)
    gate_grad = (dot(xo, gdo, 0, 1) + dot(xr, gdr, 0, 1)).astype(BF16)
    up_grad = (dot(xo, udo, 0, 1) + dot(xr, udr, 0, 1)).astype(BF16)
    return (input_grad, gate_grad, up_grad, down_grad)


def solution(mesh):
    nz, ny = mesh.shape["gx"] // 2, mesh.shape["gy"] // 4
    grid = Mesh(mesh.devices.reshape(nz, 2, ny, 2, 2), AXES)
    in_specs = (P(GY, GX), P(GX, GY), P(GX, GY), P(GY, GX), P(GY, GX))
    out_specs = (P(GY, GX), P(GX, GY), P(GX, GY), P(GY, GX))
    return jax.shard_map(
        lambda *args: per_device(nz, ny, *args),
        mesh=grid,
        in_specs=in_specs,
        out_specs=out_specs,
        check_vma=False,
    )
```

```python
import jax
import jax.numpy as jnp
from jax import lax
from jax.sharding import Mesh
from jax.sharding import PartitionSpec as P

AXES = ("z", "xl", "y", "xh", "core")
GX, GY = ("z", "xl"), ("y", "xh", "core")
SCALE = 16.0
F32, BF16, F16 = jnp.float32, jnp.bfloat16, jnp.float16


def dot(a, b, ca, cb):
    return lax.dot_general(a, b, (((ca,), (cb,)), ((), ())), preferred_element_type=F32)


def swap(x, axis):
    return lax.ppermute(x, axis, [(0, 1), (1, 0)])


def tie(*arrays):
    return lax.optimization_barrier(arrays)


def turn(x, by):
    n = x.shape[0]
    return lax.dynamic_slice_in_dim(jnp.concatenate([x, x], axis=0), by, n, axis=0)


def per_device(nz, ny, x, wg, wu, wd, c):
    rows, width = x.shape
    fwidth = wg.shape[1]
    zf = fwidth // nz
    z = lax.axis_index("z")
    right = [(i, (i + 1) % nz) for i in range(nz)]
    left = [(i, (i - 1) % nz) for i in range(nz)]

    pair = jnp.concatenate([x, c], axis=1)
    pair = jnp.broadcast_to(pair[None], (2 * ny,) + pair.shape)
    pair = lax.all_to_all(pair, ("y", "xh"), 0, 0, tiled=True).reshape(2 * ny * rows, 2 * width)
    xs, cs = pair[:, :width], pair[:, width:]
    half = xs.shape[0]

    def by_z(*weights):
        return turn(jnp.stack([w.reshape(nz, zf, width) for w in weights], axis=1), z).reshape(nz, -1, width)

    wgu = by_z(wg.T, swap(wg, "core").T, wu.T, swap(wu, "core").T)
    wdd = by_z(wd, swap(wd, "core"))
    gu = (dot(wgu.reshape(-1, width), xs, 1, 1) * SCALE).reshape(nz, 4 * zf, half)
    hg = (dot(wdd.reshape(-1, width), cs, 1, 1) * SCALE).reshape(nz, 2 * zf, half)

    def part(k):
        return jnp.concatenate([gu[k], hg[k]], axis=0)

    far = nz // 2
    cut = 3 * zf
    r = lax.ppermute(part(far)[:cut].astype(F16), "z", right).astype(F32)
    l = lax.ppermute(part(far)[cut:].astype(F16), "z", left).astype(F32)
    r = jnp.pad(r, ((0, cut), (0, 0)))
    l = jnp.pad(l, ((cut, 0), (0, 0)))
    for k in range(far - 1, 0, -1):
        r = lax.ppermute((part(k) + r).astype(F16), "z", right).astype(F32)
        l = lax.ppermute((part(nz - k) + l).astype(F16), "z", left).astype(F32)
    total = part(0) + r + l
    total = (total + swap(total.astype(F16), "xl").astype(F32)) * (1.0 / SCALE)
    gate, upper, hidden_grad = total[: 2 * zf], total[2 * zf : 4 * zf], total[4 * zf :]

    sig = jax.nn.sigmoid(gate)
    hidden = (gate * sig * upper).astype(BF16)
    gate_delta = (hidden_grad * upper * sig * (1.0 + gate * (1.0 - sig))).astype(BF16)
    up_delta = (hidden_grad * gate * sig).astype(BF16)

    chunk = [None] * nz
    chunk[0] = jnp.concatenate([gate_delta, up_delta, hidden], axis=0)
    for k in range(1, far):
        chunk[nz - k] = lax.ppermute(chunk[(nz - k + 1) % nz], "z", right)
        chunk[k] = lax.ppermute(chunk[k - 1], "z", left)
    chunk[far] = jnp.concatenate(
        [
            lax.ppermute(chunk[far + 1][:cut], "z", right),
            lax.ppermute(chunk[far - 1][cut:], "z", left),
        ],
        axis=0,
    )
    total = jnp.zeros((half, width), F32)
    for k in [0] + [j for i in range(1, far) for j in (nz - i, i)] + [far]:
        total = total + dot(chunk[k][: 4 * zf], wgu[k], 0, 0)
    total = total.astype(BF16).reshape(2 * ny, rows, width)
    total, *chunk = tie(total, *chunk)
    input_grad = lax.all_to_all(total, ("y", "xh"), 0, 0, tiled=True).astype(F32).sum(0).astype(BF16)

    deltas = jnp.concatenate([t[: 4 * zf] for t in chunk], axis=0)
    hidden = jnp.concatenate([t[4 * zf :] for t in chunk], axis=0)

    def both_cores(grads, n):
        grads = grads.reshape(nz, n, 2, zf, width)
        grads = (grads[:, :, 0] + swap(grads[:, :, 1], "core")).astype(BF16)
        grads = turn(grads, (nz - z) % nz)
        return [grads[:, i].reshape(fwidth, width) for i in range(n)]

    gate_grad, up_grad = both_cores(dot(deltas, xs, 1, 0), 2)
    (down_grad,) = both_cores(dot(hidden, cs, 1, 0), 1)
    return (input_grad, gate_grad.T, up_grad.T, down_grad)


def solution(mesh):
    nz, ny = mesh.shape["gx"] // 2, mesh.shape["gy"] // 4
    grid = Mesh(mesh.devices.reshape(nz, 2, ny, 2, 2), AXES)
    in_specs = (P(GY, GX), P(GX, GY), P(GX, GY), P(GY, GX), P(GY, GX))
    out_specs = (P(GY, GX), P(GX, GY), P(GX, GY), P(GY, GX))
    return jax.shard_map(
        lambda *args: per_device(nz, ny, *args),
        mesh=grid,
        in_specs=in_specs,
        out_specs=out_specs,
        check_vma=False,
    )
```

```python
import functools

import jax
import jax.numpy as jnp
from jax import lax
from jax.experimental import pallas as pl
from jax.experimental.pallas import tpu as pltpu
from jax.sharding import Mesh
from jax.sharding import PartitionSpec as P

AXES = ("z", "xl", "y", "xh", "core")
GX, GY = ("z", "xl"), ("y", "xh", "core")
SCALE = 16.0
F32, BF16, F16 = jnp.float32, jnp.bfloat16, jnp.float16


def dot(a, b, ca, cb):
    return lax.dot_general(a, b, (((ca,), (cb,)), ((), ())), preferred_element_type=F32)


def swap(x, axis):
    return lax.ppermute(x, axis, [(0, 1), (1, 0)])


def tie(*arrays):
    return lax.optimization_barrier(arrays)


def turn(x, by):
    n = x.shape[0]
    return lax.dynamic_slice_in_dim(jnp.concatenate([x, x], axis=0), by, n, axis=0)


def grads_kernel(nz, zf, *refs):
    chunks, (x_ref, c_ref, own_ref, send_ref) = refs[:nz], refs[nz:]
    z = lax.axis_index("z")
    for k in range(nz):
        at = lax.rem(z + k, nz)
        gu = jnp.dot(chunks[k][: 4 * zf, :], x_ref[...], preferred_element_type=F32)
        dn = jnp.dot(chunks[k][4 * zf :, :], c_ref[...], preferred_element_type=F32)
        own_ref[at, : 2 * zf, :] = gu[: 2 * zf]
        own_ref[at, 2 * zf :, :] = dn[:zf]
        send_ref[at, : 2 * zf, :] = gu[2 * zf :].astype(BF16)
        send_ref[at, 2 * zf :, :] = dn[zf:].astype(BF16)


def weight_grads(chunks, xs, cs, zf):
    shape = (len(chunks), 3 * zf, xs.shape[1])
    return pl.pallas_call(
        functools.partial(grads_kernel, len(chunks), zf),
        out_shape=(jax.ShapeDtypeStruct(shape, F32), jax.ShapeDtypeStruct(shape, BF16)),
        compiler_params=pltpu.CompilerParams(vmem_limit_bytes=40 * 2**20),
    )(*chunks, xs, cs)


def finish_kernel(zf, own_ref, got_ref, gate_ref, up_ref, down_ref):
    both = (own_ref[...] + got_ref[...].astype(F32)).astype(BF16)
    gate_ref[...] = jnp.concatenate([both[0, :zf], both[1, :zf]], axis=0).T
    up_ref[...] = jnp.concatenate([both[0, zf : 2 * zf], both[1, zf : 2 * zf]], axis=0).T
    down_ref[...] = jnp.concatenate([both[0, 2 * zf :], both[1, 2 * zf :]], axis=0)


def finish(own, got):
    nz, n, width = own.shape
    zf = n // 3
    block = pl.BlockSpec((2, n, width), lambda i: (i, 0, 0))
    across = pl.BlockSpec((width, 2 * zf), lambda i: (0, i))
    return pl.pallas_call(
        functools.partial(finish_kernel, zf),
        grid=(nz // 2,),
        in_specs=[block, block],
        out_specs=[across, across, pl.BlockSpec((2 * zf, width), lambda i: (i, 0))],
        out_shape=[
            jax.ShapeDtypeStruct((width, nz * zf), BF16),
            jax.ShapeDtypeStruct((width, nz * zf), BF16),
            jax.ShapeDtypeStruct((nz * zf, width), BF16),
        ],
    )(own, got)


def per_device(nz, ny, x, wg, wu, wd, c):
    rows, width = x.shape
    fwidth = wg.shape[1]
    zf = fwidth // nz
    z = lax.axis_index("z")
    right = [(i, (i + 1) % nz) for i in range(nz)]
    left = [(i, (i - 1) % nz) for i in range(nz)]

    pair = jnp.concatenate([x, c], axis=1)
    pair = jnp.broadcast_to(pair[None], (ny,) + pair.shape)
    pair = lax.all_to_all(pair, "y", 0, 0, tiled=True).reshape(ny * rows, 2 * width)
    pair = jnp.concatenate([pair, swap(pair, "xh")], axis=0)
    xs, cs = pair[:, :width], pair[:, width:]
    half = xs.shape[0]

    def by_z(*weights):
        return turn(jnp.stack([w.reshape(nz, zf, width) for w in weights], axis=1), z).reshape(nz, -1, width)

    wgu = by_z(wg.T, wu.T, swap(wg, "core").T, swap(wu, "core").T)
    wdd = by_z(wd, swap(wd, "core"))
    far = nz // 2


    def part_far():
        return dot(wgu[far], xs, 1, 1) * SCALE, dot(wdd[far], cs, 1, 1) * SCALE

    gu = (dot(wgu.reshape(-1, width), xs, 1, 1) * SCALE).reshape(nz, 4 * zf, half)
    hg = (dot(wdd.reshape(-1, width), cs, 1, 1) * SCALE).reshape(nz, 2 * zf, half)

    def part(k):
        return jnp.concatenate([gu[k], hg[k]], axis=0)

    cut = 3 * zf
    first = jnp.concatenate(part_far(), axis=0).astype(F16)
    r = lax.ppermute(first[:cut], "z", right).astype(F32)
    l = lax.ppermute(first[cut:], "z", left).astype(F32)
    r = jnp.pad(r, ((0, cut), (0, 0)))
    l = jnp.pad(l, ((cut, 0), (0, 0)))
    for k in range(far - 1, 0, -1):
        r = lax.ppermute((part(k) + r).astype(F16), "z", right).astype(F32)
        l = lax.ppermute((part(nz - k) + l).astype(F16), "z", left).astype(F32)
    total = part(0) + r + l
    total = (total + swap(total.astype(F16), "xl").astype(F32)) * (1.0 / SCALE)
    gate_upper = total[: 4 * zf].reshape(2, 2, zf, half)
    gate, upper = gate_upper[:, 0], gate_upper[:, 1]
    hidden_grad = total[4 * zf :].reshape(2, zf, half)

    sig = jax.nn.sigmoid(gate)
    hidden = (gate * sig * upper).astype(BF16)
    gate_delta = (hidden_grad * upper * sig * (1.0 + gate * (1.0 - sig))).astype(BF16)
    up_delta = (hidden_grad * gate * sig).astype(BF16)

    chunk = [None] * nz
    deltas = jnp.stack([gate_delta, up_delta], axis=1).reshape(4 * zf, half)
    chunk[0] = jnp.concatenate([deltas, hidden.reshape(2 * zf, half)], axis=0)
    for k in range(1, far):
        chunk[nz - k] = lax.ppermute(chunk[(nz - k + 1) % nz], "z", right)
        chunk[k] = lax.ppermute(chunk[k - 1], "z", left)
    chunk[far] = jnp.concatenate(
        [
            lax.ppermute(chunk[far + 1][:cut], "z", right),
            lax.ppermute(chunk[far - 1][cut:], "z", left),
        ],
        axis=0,
    )
    total = jnp.zeros((half, width), F32)
    for k in [0] + [j for i in range(1, far) for j in (nz - i, i)] + [far]:
        total = total + dot(chunk[k][: 4 * zf], wgu[k], 0, 0)

    total, send, *chunk = tie(total[: half // 2], total[half // 2 :].astype(BF16), *chunk)
    got = swap(send, "xh")
    own, send = weight_grads(chunk, xs, cs, zf)
    got, own, send = tie(got, own, send)
    total = (total + got.astype(F32)).astype(BF16).reshape(ny, rows, width)
    recv = lax.all_to_all(total, "y", 0, 0, tiled=True)
    gate_grad, up_grad, down_grad = finish(own, swap(send, "core"))
    recv, gate_grad, up_grad, down_grad = tie(recv, gate_grad, up_grad, down_grad)
    input_grad = recv.astype(F32).sum(0).astype(BF16)
    return (input_grad, gate_grad, up_grad, down_grad)


def solution(mesh):
    nz, ny = mesh.shape["gx"] // 2, mesh.shape["gy"] // 4
    grid = Mesh(mesh.devices.reshape(nz, 2, ny, 2, 2), AXES)
    in_specs = (P(GY, GX), P(GX, GY), P(GX, GY), P(GY, GX), P(GY, GX))
    out_specs = (P(GY, GX), P(GX, GY), P(GX, GY), P(GY, GX))
    return jax.shard_map(
        lambda *args: per_device(nz, ny, *args),
        mesh=grid,
        in_specs=in_specs,
        out_specs=out_specs,
        check_vma=False,
    )
```

```python
import functools

import jax
import jax.numpy as jnp
from jax import lax
from jax.experimental import pallas as pl
from jax.experimental.pallas import tpu as pltpu
from jax.sharding import Mesh
from jax.sharding import PartitionSpec as P

AXES = ("z", "xl", "y", "xh", "core")
GX, GY = ("z", "xl"), ("y", "xh", "core")
SCALE = 16.0
F32, BF16, F16 = jnp.float32, jnp.bfloat16, jnp.float16


def dot(a, b, ca, cb):
    return lax.dot_general(a, b, (((ca,), (cb,)), ((), ())), preferred_element_type=F32)


def swap(x, axis):
    return lax.ppermute(x, axis, [(0, 1), (1, 0)])


def tie(*arrays):
    return lax.optimization_barrier(arrays)


def turn(x, by):
    n = x.shape[0]
    return lax.dynamic_slice_in_dim(jnp.concatenate([x, x], axis=0), by, n, axis=0)


def grads_kernel(nz, zf, *refs):
    chunks, (x_ref, c_ref, own_ref, send_ref) = refs[:nz], refs[nz:]
    z = lax.axis_index("z")
    for k in range(nz):
        at = lax.rem(z + k, nz)
        gu = jnp.dot(chunks[k][: 4 * zf, :], x_ref[...], preferred_element_type=F32)
        dn = jnp.dot(chunks[k][4 * zf :, :], c_ref[...], preferred_element_type=F32)
        own_ref[at, : 2 * zf, :] = gu[: 2 * zf]
        own_ref[at, 2 * zf :, :] = dn[:zf]
        send_ref[at, : 2 * zf, :] = gu[2 * zf :].astype(BF16)
        send_ref[at, 2 * zf :, :] = dn[zf:].astype(BF16)


def input_kernel(nz, at, *refs):
    chunks, (own_ref, oth_ref, out_ref) = refs[:nz], refs[nz:]
    n, h = out_ref.shape[0], own_ref.shape[1]
    total = jnp.zeros(out_ref.shape, F32)
    for k in range(nz):
        for i, ref in enumerate((own_ref, oth_ref)):
            deltas = chunks[k][i * h : (i + 1) * h, at : at + n]
            total += lax.dot_general(
                deltas, ref[k], (((0,), (0,)), ((), ())), preferred_element_type=F32
            )
    out_ref[...] = total.astype(out_ref.dtype)


def input_grads(chunks, own, oth, at, n, dtype):
    return pl.pallas_call(
        functools.partial(input_kernel, len(chunks), at),
        out_shape=jax.ShapeDtypeStruct((n, own.shape[2]), dtype),
        compiler_params=pltpu.CompilerParams(vmem_limit_bytes=40 * 2**20),
    )(*chunks, own, oth)


def weight_grads(chunks, xs, cs, zf):
    shape = (len(chunks), 3 * zf, xs.shape[1])
    return pl.pallas_call(
        functools.partial(grads_kernel, len(chunks), zf),
        out_shape=(jax.ShapeDtypeStruct(shape, F32), jax.ShapeDtypeStruct(shape, BF16)),
        compiler_params=pltpu.CompilerParams(vmem_limit_bytes=40 * 2**20),
    )(*chunks, xs, cs)


def finish_kernel(zf, own_ref, got_ref, gate_ref, up_ref, down_ref):
    for i in range(0, own_ref.shape[0], 2):
        both = (own_ref[i : i + 2] + got_ref[i : i + 2].astype(F32)).astype(BF16)
        at = pl.ds(i * zf, 2 * zf)
        gate_ref[:, at] = jnp.concatenate([both[0, :zf], both[1, :zf]], axis=0).T
        up_ref[:, at] = jnp.concatenate([both[0, zf : 2 * zf], both[1, zf : 2 * zf]], axis=0).T
        down_ref[at, :] = jnp.concatenate([both[0, 2 * zf :], both[1, 2 * zf :]], axis=0)


def finish(own, got):
    nz, n, width = own.shape
    zf = n // 3
    return pl.pallas_call(
        functools.partial(finish_kernel, zf),
        out_shape=[
            jax.ShapeDtypeStruct((width, nz * zf), BF16),
            jax.ShapeDtypeStruct((width, nz * zf), BF16),
            jax.ShapeDtypeStruct((nz * zf, width), BF16),
        ],
        compiler_params=pltpu.CompilerParams(vmem_limit_bytes=40 * 2**20),
    )(own, got)


def turn(x, by):
    n = x.shape[0]
    return lax.dynamic_slice_in_dim(jnp.concatenate([x, x], axis=0), by, n, axis=0)


def grads_kernel(nz, zf, *refs):
    chunks, (x_ref, c_ref, own_ref, send_ref) = refs[:nz], refs[nz:]
    z = lax.axis_index("z")
    for k in range(nz):
        at = lax.rem(z + k, nz)
        gu = jnp.dot(chunks[k][: 4 * zf, :], x_ref[...], preferred_element_type=F32)
        dn = jnp.dot(chunks[k][4 * zf :, :], c_ref[...], preferred_element_type=F32)
        own_ref[at, : 2 * zf, :] = gu[: 2 * zf]
        own_ref[at, 2 * zf :, :] = dn[:zf]
        send_ref[at, : 2 * zf, :] = gu[2 * zf :].astype(BF16)
        send_ref[at, 2 * zf :, :] = dn[zf:].astype(BF16)


def input_kernel(nz, at, *refs):
    chunks, (own_ref, oth_ref, out_ref) = refs[:nz], refs[nz:]
    n, h = out_ref.shape[0], own_ref.shape[1]
    total = jnp.zeros(out_ref.shape, F32)
    for k in range(nz):
        for i, ref in enumerate((own_ref, oth_ref)):
            deltas = chunks[k][i * h : (i + 1) * h, at : at + n]
            total += lax.dot_general(
                deltas, ref[k], (((0,), (0,)), ((), ())), preferred_element_type=F32
            )
    out_ref[...] = total.astype(out_ref.dtype)


def input_grads(chunks, own, oth, at, n, dtype):
    return pl.pallas_call(
        functools.partial(input_kernel, len(chunks), at),
        out_shape=jax.ShapeDtypeStruct((n, own.shape[2]), dtype),
        compiler_params=pltpu.CompilerParams(vmem_limit_bytes=40 * 2**20),
    )(*chunks, own, oth)


def weight_grads(chunks, xs, cs, zf):
    shape = (len(chunks), 3 * zf, xs.shape[1])
    return pl.pallas_call(
        functools.partial(grads_kernel, len(chunks), zf),
        out_shape=(jax.ShapeDtypeStruct(shape, F32), jax.ShapeDtypeStruct(shape, BF16)),
        compiler_params=pltpu.CompilerParams(vmem_limit_bytes=40 * 2**20),
    )(*chunks, xs, cs)


def finish_kernel(zf, own_ref, got_ref, gate_ref, up_ref, down_ref):
    both = (own_ref[...] + got_ref[...].astype(F32)).astype(BF16)
    gate_ref[...] = jnp.concatenate([both[0, :zf], both[1, :zf]], axis=0).T
    up_ref[...] = jnp.concatenate([both[0, zf : 2 * zf], both[1, zf : 2 * zf]], axis=0).T
    down_ref[...] = jnp.concatenate([both[0, 2 * zf :], both[1, 2 * zf :]], axis=0)


def finish(own, got):
    nz, n, width = own.shape
    zf = n // 3
    block = pl.BlockSpec((2, n, width), lambda i: (i, 0, 0))
    across = pl.BlockSpec((width, 2 * zf), lambda i: (0, i))
    return pl.pallas_call(
        functools.partial(finish_kernel, zf),
        grid=(nz // 2,),
        in_specs=[block, block],
        out_specs=[across, across, pl.BlockSpec((2 * zf, width), lambda i: (i, 0))],
        out_shape=[
            jax.ShapeDtypeStruct((width, nz * zf), BF16),
            jax.ShapeDtypeStruct((width, nz * zf), BF16),
            jax.ShapeDtypeStruct((nz * zf, width), BF16),
        ],
    )(own, got)


def per_device(nz, ny, x, wg, wu, wd, c):
    rows, width = x.shape
    fwidth = wg.shape[1]
    zf = fwidth // nz
    z = lax.axis_index("z")
    right = [(i, (i + 1) % nz) for i in range(nz)]
    left = [(i, (i - 1) % nz) for i in range(nz)]

    pair = jnp.concatenate([x, c], axis=1)
    pair = jnp.broadcast_to(pair[None], (ny,) + pair.shape)
    pair = lax.all_to_all(pair, "y", 0, 0, tiled=True).reshape(ny * rows, 2 * width)
    other = swap(pair, "xh")
    part_tokens = pair.shape[0]
    x0, c0, x1, c1 = pair[:, :width], pair[:, width:], other[:, :width], other[:, width:]
    xs, cs = jnp.concatenate([x0, x1], axis=0), jnp.concatenate([c0, c1], axis=0)
    half = 2 * part_tokens

    def by_z(*weights):
        return turn(jnp.stack([w.reshape(nz, zf, width) for w in weights], axis=1), z).reshape(nz, -1, width)

    gu_own, gu_oth = by_z(wg.T, wu.T), by_z(swap(wg, "core").T, swap(wu, "core").T)
    d_own, d_oth = by_z(wd), by_z(swap(wd, "core"))
    far = nz // 2

    def part_far(t, u):
        halves = [(gu_own, t), (gu_oth, t), (d_own, u), (d_oth, u)]
        return jnp.concatenate([dot(w[far], v, 1, 1) for w, v in halves], axis=0) * SCALE

    parts = [
        (dot(w.reshape(-1, width), t, 1, 1) * SCALE).reshape(nz, -1, half)
        for w, t in ((gu_own, xs), (gu_oth, xs), (d_own, cs), (d_oth, cs))
    ]

    def part(k):
        return jnp.concatenate([p[k] for p in parts], axis=0)

    r = lax.ppermute(part_far(x0, c0).astype(F16), "z", right).astype(F32)
    l = lax.ppermute(part_far(x1, c1).astype(F16), "z", left).astype(F32)
    r = jnp.pad(r, ((0, 0), (0, part_tokens)))
    l = jnp.pad(l, ((0, 0), (part_tokens, 0)))
    for k in range(far - 1, 0, -1):
        r = lax.ppermute((part(k) + r).astype(F16), "z", right).astype(F32)
        l = lax.ppermute((part(nz - k) + l).astype(F16), "z", left).astype(F32)
    total = part(0) + r + l
    total = (total + swap(total.astype(F16), "xl").astype(F32)) * (1.0 / SCALE)
    gate_upper = total[: 4 * zf].reshape(2, 2, zf, half)
    gate, upper = gate_upper[:, 0], gate_upper[:, 1]
    hidden_grad = total[4 * zf :].reshape(2, zf, half)

    sig = jax.nn.sigmoid(gate)
    hidden = (gate * sig * upper).astype(BF16)
    gate_delta = (hidden_grad * upper * sig * (1.0 + gate * (1.0 - sig))).astype(BF16)
    up_delta = (hidden_grad * gate * sig).astype(BF16)

    chunk = [None] * nz
    deltas = jnp.stack([gate_delta, up_delta], axis=1).reshape(4 * zf, half)
    chunk[0] = jnp.concatenate([deltas, hidden.reshape(2 * zf, half)], axis=0)
    for k in range(1, far):
        chunk[nz - k] = lax.ppermute(chunk[(nz - k + 1) % nz], "z", right)
        chunk[k] = lax.ppermute(chunk[k - 1], "z", left)
    chunk[far] = jnp.concatenate(
        [
            lax.ppermute(chunk[far + 1][:, :part_tokens], "z", right),
            lax.ppermute(chunk[far - 1][:, part_tokens:], "z", left),
        ],
        axis=1,
    )

    send = input_grads(chunk, gu_own, gu_oth, part_tokens, part_tokens, BF16)
    send, *chunk = tie(send, *chunk)
    got = swap(send, "xh")
    own, send = weight_grads(chunk, xs, cs, zf)
    total = input_grads(chunk, gu_own, gu_oth, 0, part_tokens, F32)
    got, total = tie(got, total)
    total = (total + got.astype(F32)).astype(BF16).reshape(ny, rows, width)
    total, own, send = tie(total, own, send)
    recv = lax.all_to_all(total, "y", 0, 0, tiled=True)
    gate_grad, up_grad, down_grad = finish(own, swap(send, "core"))
    recv, gate_grad, up_grad, down_grad = tie(recv, gate_grad, up_grad, down_grad)
    input_grad = recv.astype(F32).sum(0).astype(BF16)
    return (input_grad, gate_grad, up_grad, down_grad)


def solution(mesh):
    nz, ny = mesh.shape["gx"] // 2, mesh.shape["gy"] // 4
    grid = Mesh(mesh.devices.reshape(nz, 2, ny, 2, 2), AXES)
    in_specs = (P(GY, GX), P(GX, GY), P(GX, GY), P(GY, GX), P(GY, GX))
    out_specs = (P(GY, GX), P(GX, GY), P(GX, GY), P(GY, GX))
    return jax.shard_map(
        lambda *args: per_device(nz, ny, *args),
        mesh=grid,
        in_specs=in_specs,
        out_specs=out_specs,
        check_vma=False,
    )
```

```python
import functools

import jax
import jax.numpy as jnp
from jax import lax
from jax.experimental import pallas as pl
from jax.experimental.pallas import tpu as pltpu
from jax.sharding import Mesh
from jax.sharding import PartitionSpec as P

AXES = ("z", "xl", "y", "xh", "core")
GX, GY = ("z", "xl"), ("y", "xh", "core")
SCALE = 16.0
F32, BF16, F16 = jnp.float32, jnp.bfloat16, jnp.float16


def dot(a, b, ca, cb):
    return lax.dot_general(a, b, (((ca,), (cb,)), ((), ())), preferred_element_type=F32)


def swap(x, axis):
    return lax.ppermute(x, axis, [(0, 1), (1, 0)])


def tie(*arrays):
    return lax.optimization_barrier(arrays)


def turn(x, by):
    n = x.shape[0]
    return lax.dynamic_slice_in_dim(jnp.concatenate([x, x], axis=0), by, n, axis=0)


def input_kernel(nz, at, *refs):
    chunks, (own_ref, oth_ref, out_ref) = refs[:nz], refs[nz:]
    n, h, step = out_ref.shape[0], own_ref.shape[1], chunks[0].shape[0] // 2
    total = jnp.zeros(out_ref.shape, F32)
    for k in range(nz):
        for i, ref in enumerate((own_ref, oth_ref)):
            deltas = chunks[k][i * step : i * step + h, at : at + n]
            total += lax.dot_general(
                deltas, ref[k], (((0,), (0,)), ((), ())), preferred_element_type=F32
            )
    out_ref[...] = total.astype(out_ref.dtype)


def input_grads(chunks, own, oth, at, n, dtype):
    return pl.pallas_call(
        functools.partial(input_kernel, len(chunks), at),
        out_shape=jax.ShapeDtypeStruct((n, own.shape[2]), dtype),
        compiler_params=pltpu.CompilerParams(vmem_limit_bytes=40 * 2**20),
    )(*chunks, own, oth)


def grads_kernel(order, zf, *refs):
    nz = len(order)
    chunks, (got_ref, x_ref, c_ref, xo_ref, co_ref, gate_ref, up_ref, down_ref, sums) = refs[:nz], refs[nz:]
    z = lax.axis_index("z")
    n = 2 * zf
    for k in range(nz):
        gu = jnp.dot(chunks[k][:n, :], x_ref[...], preferred_element_type=F32)
        gu += jnp.dot(got_ref[k, :n, :], xo_ref[...], preferred_element_type=F32)
        dn = jnp.dot(chunks[k][n : n + zf, :], c_ref[...], preferred_element_type=F32)
        dn += jnp.dot(got_ref[k, n:, :], co_ref[...], preferred_element_type=F32)
        at = lax.rem(z + order[k], nz)
        sums[at, :n, :] = gu.astype(BF16)
        sums[at, n:, :] = dn.astype(BF16)
    for i in range(0, nz, 2):
        at = pl.ds(i * zf, 2 * zf)
        gate_ref[:, at] = jnp.concatenate([sums[i, :zf, :], sums[i + 1, :zf, :]], axis=0).T
        up_ref[:, at] = jnp.concatenate([sums[i, zf:n, :], sums[i + 1, zf:n, :]], axis=0).T
        down_ref[at, :] = jnp.concatenate([sums[i, n:, :], sums[i + 1, n:, :]], axis=0)


def weight_grads(chunks, order, got, tokens, zf):
    nz, width = len(chunks), tokens[0].shape[1]
    return pl.pallas_call(
        functools.partial(grads_kernel, order, zf),
        out_shape=[
            jax.ShapeDtypeStruct((width, nz * zf), BF16),
            jax.ShapeDtypeStruct((width, nz * zf), BF16),
            jax.ShapeDtypeStruct((nz * zf, width), BF16),
        ],
        scratch_shapes=[pltpu.VMEM((nz, 3 * zf, width), BF16)],
        compiler_params=pltpu.CompilerParams(vmem_limit_bytes=40 * 2**20),
    )(*chunks, got, *tokens)


def per_device(nz, ny, x, wg, wu, wd, c):
    rows, width = x.shape
    fwidth = wg.shape[1]
    zf = fwidth // nz
    z = lax.axis_index("z")
    right = [(i, (i + 1) % nz) for i in range(nz)]
    left = [(i, (i - 1) % nz) for i in range(nz)]

    pair = jnp.concatenate([x, c], axis=1)
    pair = jnp.broadcast_to(pair[None], (ny,) + pair.shape)
    pair = lax.all_to_all(pair, "y", 0, 0, tiled=True).reshape(ny * rows, 2 * width)
    pair, wg_oth, wu_oth, wd_oth = tie(pair, swap(wg, "core"), swap(wu, "core"), swap(wd, "core"))
    other = swap(pair, "xh")
    part_tokens = pair.shape[0]
    x0, c0 = pair[:, :width], pair[:, width:]
    half = 2 * part_tokens

    def by_z(*weights):
        return turn(jnp.stack([w.reshape(nz, zf, width) for w in weights], axis=1), z).reshape(nz, -1, width)

    gu_own, gu_oth = by_z(wg.T, wu.T), by_z(wg_oth.T, wu_oth.T)
    d_own, d_oth = by_z(wd), by_z(wd_oth)
    far = nz // 2

    def part_far(t, u):
        halves = [(gu_own, t), (d_own, u), (gu_oth, t), (d_oth, u)]
        return jnp.concatenate([dot(w[far], v, 1, 1) for w, v in halves], axis=0) * SCALE

    def products(t, u):
        pairs = ((gu_own, t), (d_own, u), (gu_oth, t), (d_oth, u))
        return [(dot(w.reshape(-1, width), v, 1, 1) * SCALE).reshape(nz, -1, part_tokens) for w, v in pairs]

    first = products(x0, c0)
    other, *first = tie(other, *first)
    x1, c1 = other[:, :width], other[:, width:]
    xs, cs = jnp.concatenate([x0, x1], axis=0), jnp.concatenate([c0, c1], axis=0)
    parts = list(zip(first, products(x1, c1)))

    def half_part(i, k):
        return jnp.concatenate([p[i][k] for p in parts], axis=0)

    def part(k):
        return jnp.concatenate([half_part(0, k), half_part(1, k)], axis=1)

    r = lax.ppermute(part_far(x0, c0).astype(F16), "z", right).astype(F32)
    l = lax.ppermute(half_part(1, far).astype(F16), "z", left).astype(F32)
    r = jnp.pad(r, ((0, 0), (0, part_tokens)))
    l = jnp.pad(l, ((0, 0), (part_tokens, 0)))
    for k in range(far - 1, 0, -1):
        r = lax.ppermute((part(k) + r).astype(F16), "z", right).astype(F32)
        l = lax.ppermute((part(nz - k) + l).astype(F16), "z", left).astype(F32)
    total = part(0) + r + l
    got = swap(total.astype(F16), "xl")
    tokens_oth = swap(jnp.stack([xs, cs]), "core")
    got, tokens_oth = tie(got, tokens_oth)
    total = ((total + got.astype(F32)) * (1.0 / SCALE)).reshape(2, 3, zf, half)
    gate, upper, hidden_grad = total[:, 0], total[:, 1], total[:, 2]

    sig = jax.nn.sigmoid(gate)
    hidden = (gate * sig * upper).astype(BF16)
    gate_delta = (hidden_grad * upper * sig * (1.0 + gate * (1.0 - sig))).astype(BF16)
    up_delta = (hidden_grad * gate * sig).astype(BF16)

    chunk = [None] * nz
    chunk[0] = jnp.stack([gate_delta, up_delta, hidden], axis=1).reshape(6 * zf, half)
    for k in range(1, far):
        chunk[nz - k] = lax.ppermute(chunk[(nz - k + 1) % nz], "z", right)
        chunk[k] = lax.ppermute(chunk[k - 1], "z", left)
    chunk[far] = jnp.concatenate(
        [
            lax.ppermute(chunk[far + 1][:, :part_tokens], "z", right),
            lax.ppermute(chunk[far - 1][:, part_tokens:], "z", left),
        ],
        axis=1,
    )

    order = [0] + [j for i in range(1, far) for j in (nz - i, i)] + [far]
    deltas = jnp.stack([chunk[k][3 * zf :] for k in order[:-1]])
    chunk[far], deltas = tie(chunk[far], deltas)
    send = input_grads(chunk, gu_own, gu_oth, part_tokens, part_tokens, BF16)
    send, *chunk = tie(send, *chunk)
    got = swap(send, "xh")
    total = input_grads(chunk, gu_own, gu_oth, 0, part_tokens, F32)
    deltas = jnp.concatenate([deltas, chunk[far][None, 3 * zf :]], axis=0)
    got, total, deltas = tie(got, total, deltas)
    deltas = swap(deltas, "core")
    total = (total + got.astype(F32)).astype(BF16).reshape(ny, rows, width)
    recv = lax.all_to_all(total, "y", 0, 0, tiled=True)
    tokens = (xs, cs, tokens_oth[0], tokens_oth[1])
    gate_grad, up_grad, down_grad = weight_grads([chunk[k] for k in order], order, deltas, tokens, zf)
    recv, gate_grad, up_grad, down_grad = tie(recv, gate_grad, up_grad, down_grad)
    input_grad = recv.astype(F32).sum(0).astype(BF16)
    return (input_grad, gate_grad, up_grad, down_grad)


def solution(mesh):
    nz, ny = mesh.shape["gx"] // 2, mesh.shape["gy"] // 4
    grid = Mesh(mesh.devices.reshape(nz, 2, ny, 2, 2), AXES)
    in_specs = (P(GY, GX), P(GX, GY), P(GX, GY), P(GY, GX), P(GY, GX))
    out_specs = (P(GY, GX), P(GX, GY), P(GX, GY), P(GY, GX))
    return jax.shard_map(
        lambda *args: per_device(nz, ny, *args),
        mesh=grid,
        in_specs=in_specs,
        out_specs=out_specs,
        check_vma=False,
    )
```

```python
import functools

import jax
import jax.numpy as jnp
from jax import lax
from jax.experimental import pallas as pl
from jax.experimental.pallas import tpu as pltpu
from jax.sharding import Mesh
from jax.sharding import PartitionSpec as P

AXES = ("z", "xl", "y", "xh", "core")
GX, GY = ("z", "xl"), ("y", "xh", "core")
SCALE = 16.0
F32, BF16, F16 = jnp.float32, jnp.bfloat16, jnp.float16


def dot(a, b, ca, cb):
    return lax.dot_general(a, b, (((ca,), (cb,)), ((), ())), preferred_element_type=F32)


def swap(x, axis):
    return lax.ppermute(x, axis, [(0, 1), (1, 0)])


def tie(*arrays):
    return lax.optimization_barrier(arrays)


def order_kernel(nz, g_ref, u_ref, d_ref, gu_out, d_out):
    z = lax.axis_index("z")
    n = d_ref.shape[0] // nz
    gate, up = g_ref[...].T, u_ref[...].T
    for i in range(nz):
        k = lax.rem(i + nz - z, nz)
        gu_out[k, :n, :] = gate[i * n : (i + 1) * n]
        gu_out[k, n:, :] = up[i * n : (i + 1) * n]
        d_out[k, :, :] = d_ref[i * n : (i + 1) * n, :]


def in_order(nz, wg, wu, wd):
    n, width = wd.shape[0] // nz, wd.shape[1]
    return pl.pallas_call(
        functools.partial(order_kernel, nz),
        out_shape=[
            jax.ShapeDtypeStruct((nz, 2 * n, width), wd.dtype),
            jax.ShapeDtypeStruct((nz, n, width), wd.dtype),
        ],
        compiler_params=pltpu.CompilerParams(vmem_limit_bytes=40 * 2**20),
    )(wg, wu, wd)


def input_kernel(nz, at, *refs):
    chunks, (own_ref, oth_ref, out_ref) = refs[:nz], refs[nz:]
    n, h, step = out_ref.shape[0], own_ref.shape[1], chunks[0].shape[0] // 2
    total = jnp.zeros(out_ref.shape, F32)
    for k in range(nz):
        for i, ref in enumerate((own_ref, oth_ref)):
            deltas = chunks[k][i * step : i * step + h, at : at + n]
            total += lax.dot_general(
                deltas, ref[k], (((0,), (0,)), ((), ())), preferred_element_type=F32
            )
    out_ref[...] = total.astype(out_ref.dtype)


def input_grads(chunks, own, oth, at, n, dtype):
    return pl.pallas_call(
        functools.partial(input_kernel, len(chunks), at),
        out_shape=jax.ShapeDtypeStruct((n, own.shape[2]), dtype),
        compiler_params=pltpu.CompilerParams(vmem_limit_bytes=40 * 2**20),
    )(*chunks, own, oth)


def grads_kernel(order, zf, *refs):
    nz = len(order)
    chunks, (got_ref, x_ref, c_ref, xo_ref, co_ref, gate_ref, up_ref, down_ref, sums) = refs[:nz], refs[nz:]
    z = lax.axis_index("z")
    n = 2 * zf
    for k in range(nz):
        gu = jnp.dot(chunks[k][:n, :], x_ref[...], preferred_element_type=F32)
        gu += jnp.dot(got_ref[k, :n, :], xo_ref[...], preferred_element_type=F32)
        dn = jnp.dot(chunks[k][n : n + zf, :], c_ref[...], preferred_element_type=F32)
        dn += jnp.dot(got_ref[k, n:, :], co_ref[...], preferred_element_type=F32)
        at = lax.rem(z + order[k], nz)
        sums[at, :n, :] = gu.astype(BF16)
        sums[at, n:, :] = dn.astype(BF16)
    for i in range(0, nz, 2):
        at = pl.ds(i * zf, 2 * zf)
        gate_ref[:, at] = jnp.concatenate([sums[i, :zf, :], sums[i + 1, :zf, :]], axis=0).T
        up_ref[:, at] = jnp.concatenate([sums[i, zf:n, :], sums[i + 1, zf:n, :]], axis=0).T
        down_ref[at, :] = jnp.concatenate([sums[i, n:, :], sums[i + 1, n:, :]], axis=0)


def weight_grads(chunks, order, got, tokens, zf):
    nz, width = len(chunks), tokens[0].shape[1]
    return pl.pallas_call(
        functools.partial(grads_kernel, order, zf),
        out_shape=[
            jax.ShapeDtypeStruct((width, nz * zf), BF16),
            jax.ShapeDtypeStruct((width, nz * zf), BF16),
            jax.ShapeDtypeStruct((nz * zf, width), BF16),
        ],
        scratch_shapes=[pltpu.VMEM((nz, 3 * zf, width), BF16)],
        compiler_params=pltpu.CompilerParams(vmem_limit_bytes=40 * 2**20),
    )(*chunks, got, *tokens)


def per_device(nz, ny, x, wg, wu, wd, c):
    rows, width = x.shape
    fwidth = wg.shape[1]
    zf = fwidth // nz
    z = lax.axis_index("z")
    right = [(i, (i + 1) % nz) for i in range(nz)]
    left = [(i, (i - 1) % nz) for i in range(nz)]

    pair = jnp.concatenate([x, c], axis=1)
    pair = jnp.broadcast_to(pair[None], (ny,) + pair.shape)
    pair = lax.all_to_all(pair, "y", 0, 0, tiled=True).reshape(ny * rows, 2 * width)
    other = swap(pair, "xh")
    part_tokens = pair.shape[0]
    x0, c0 = pair[:, :width], pair[:, width:]
    half = 2 * part_tokens

    gu_own, d_own = in_order(nz, wg, wu, wd)
    gu_oth, d_oth = in_order(nz, swap(wg, "core"), swap(wu, "core"), swap(wd, "core"))
    far = nz // 2

    def part_far(t, u):
        halves = [(gu_own, t), (d_own, u), (gu_oth, t), (d_oth, u)]
        return jnp.concatenate([dot(w[far], v, 1, 1) for w, v in halves], axis=0) * SCALE

    def products(t, u):
        pairs = ((gu_own, t), (d_own, u), (gu_oth, t), (d_oth, u))
        return [(dot(w.reshape(-1, width), v, 1, 1) * SCALE).reshape(nz, -1, part_tokens) for w, v in pairs]

    first = products(x0, c0)
    other, *first = tie(other, *first)
    x1, c1 = other[:, :width], other[:, width:]
    xs, cs = jnp.concatenate([x0, x1], axis=0), jnp.concatenate([c0, c1], axis=0)
    parts = list(zip(first, products(x1, c1)))

    def half_part(i, k):
        return jnp.concatenate([p[i][k] for p in parts], axis=0)

    def part(k):
        return jnp.concatenate([half_part(0, k), half_part(1, k)], axis=1)

    r = lax.ppermute(part_far(x0, c0).astype(F16), "z", right).astype(F32)
    l = lax.ppermute(half_part(1, far).astype(F16), "z", left).astype(F32)
    r = jnp.pad(r, ((0, 0), (0, part_tokens)))
    l = jnp.pad(l, ((0, 0), (part_tokens, 0)))
    for k in range(far - 1, 0, -1):
        r = lax.ppermute((part(k) + r).astype(F16), "z", right).astype(F32)
        l = lax.ppermute((part(nz - k) + l).astype(F16), "z", left).astype(F32)
    total = part(0) + r + l
    got = swap(total.astype(F16), "xl")
    tokens_oth = swap(jnp.stack([xs, cs]), "core")
    got, tokens_oth = tie(got, tokens_oth)
    total = ((total + got.astype(F32)) * (1.0 / SCALE)).reshape(2, 3, zf, half)
    gate, upper, hidden_grad = total[:, 0], total[:, 1], total[:, 2]

    sig = jax.nn.sigmoid(gate)
    hidden = (gate * sig * upper).astype(BF16)
    gate_delta = (hidden_grad * upper * sig * (1.0 + gate * (1.0 - sig))).astype(BF16)
    up_delta = (hidden_grad * gate * sig).astype(BF16)

    chunk = [None] * nz
    chunk[0] = jnp.stack([gate_delta, up_delta, hidden], axis=1).reshape(6 * zf, half)
    for k in range(1, far):
        chunk[nz - k] = lax.ppermute(chunk[(nz - k + 1) % nz], "z", right)
        chunk[k] = lax.ppermute(chunk[k - 1], "z", left)
    chunk[far] = jnp.concatenate(
        [
            lax.ppermute(chunk[far + 1][:, :part_tokens], "z", right),
            lax.ppermute(chunk[far - 1][:, part_tokens:], "z", left),
        ],
        axis=1,
    )

    order = [0] + [j for i in range(1, far) for j in (nz - i, i)] + [far]
    deltas = jnp.stack([chunk[k][3 * zf :] for k in order[:-1]])
    chunk[far], deltas = tie(chunk[far], deltas)
    send = input_grads(chunk, gu_own, gu_oth, part_tokens, part_tokens, BF16)
    send, *chunk = tie(send, *chunk)
    got = swap(send, "xh")
    total = input_grads(chunk, gu_own, gu_oth, 0, part_tokens, F32)
    deltas = jnp.concatenate([deltas, chunk[far][None, 3 * zf :]], axis=0)
    got, total, deltas = tie(got, total, deltas)
    deltas = swap(deltas, "core")
    total = (total + got.astype(F32)).astype(BF16).reshape(ny, rows, width)
    recv = lax.all_to_all(total, "y", 0, 0, tiled=True)
    tokens = (xs, cs, tokens_oth[0], tokens_oth[1])
    gate_grad, up_grad, down_grad = weight_grads([chunk[k] for k in order], order, deltas, tokens, zf)
    recv, gate_grad, up_grad, down_grad = tie(recv, gate_grad, up_grad, down_grad)
    input_grad = recv.astype(F32).sum(0).astype(BF16)
    return (input_grad, gate_grad, up_grad, down_grad)


def solution(mesh):
    nz, ny = mesh.shape["gx"] // 2, mesh.shape["gy"] // 4
    grid = Mesh(mesh.devices.reshape(nz, 2, ny, 2, 2), AXES)
    in_specs = (P(GY, GX), P(GX, GY), P(GX, GY), P(GY, GX), P(GY, GX))
    out_specs = (P(GY, GX), P(GX, GY), P(GX, GY), P(GY, GX))
    return jax.shard_map(
        lambda *args: per_device(nz, ny, *args),
        mesh=grid,
        in_specs=in_specs,
        out_specs=out_specs,
        check_vma=False,
    )
```

```python
import functools

import jax
import jax.numpy as jnp
from jax import lax
from jax.experimental import pallas as pl
from jax.experimental.pallas import tpu as pltpu
from jax.sharding import Mesh
from jax.sharding import PartitionSpec as P

AXES = ("z", "xl", "y", "xh", "core")
GX, GY = ("z", "xl"), ("y", "xh", "core")
SCALE = 16.0
F32, BF16, F16 = jnp.float32, jnp.bfloat16, jnp.float16


def dot(a, b, ca, cb):
    return lax.dot_general(a, b, (((ca,), (cb,)), ((), ())), preferred_element_type=F32)


def swap(x, axis):
    return lax.ppermute(x, axis, [(0, 1), (1, 0)])


def tie(*arrays):
    return lax.optimization_barrier(arrays)


def order_kernel(nz, g_ref, u_ref, d_ref, gu_out, d_out):
    z = lax.axis_index("z")
    n = d_ref.shape[0] // nz
    gate, up = g_ref[...].T, u_ref[...].T
    for i in range(nz):
        k = lax.rem(i + nz - z, nz)
        gu_out[k, :n, :] = gate[i * n : (i + 1) * n]
        gu_out[k, n:, :] = up[i * n : (i + 1) * n]
        d_out[k, :, :] = d_ref[i * n : (i + 1) * n, :]


def in_order(nz, wg, wu, wd):
    n, width = wd.shape[0] // nz, wd.shape[1]
    return pl.pallas_call(
        functools.partial(order_kernel, nz),
        out_shape=[
            jax.ShapeDtypeStruct((nz, 2 * n, width), wd.dtype),
            jax.ShapeDtypeStruct((nz, n, width), wd.dtype),
        ],
        compiler_params=pltpu.CompilerParams(vmem_limit_bytes=16 * 2**20),
    )(wg, wu, wd)


def input_kernel(nz, at, *refs):
    chunks, (own_ref, oth_ref, out_ref) = refs[:nz], refs[nz:]
    n, h, step = out_ref.shape[0], own_ref.shape[1], chunks[0].shape[0] // 2
    total = jnp.zeros(out_ref.shape, F32)
    for k in range(nz):
        for i, ref in enumerate((own_ref, oth_ref)):
            deltas = chunks[k][i * step : i * step + h, at : at + n]
            total += lax.dot_general(
                deltas, ref[k], (((0,), (0,)), ((), ())), preferred_element_type=F32
            )
    out_ref[...] = total.astype(out_ref.dtype)


def input_grads(chunks, own, oth, at, n, dtype):
    return pl.pallas_call(
        functools.partial(input_kernel, len(chunks), at),
        out_shape=jax.ShapeDtypeStruct((n, own.shape[2]), dtype),
        compiler_params=pltpu.CompilerParams(vmem_limit_bytes=16 * 2**20),
    )(*chunks, own, oth)


def grads_kernel(order, zf, *refs):
    nz = len(order)
    chunks, (got_ref, own_ref, oth_ref, gate_ref, up_ref, down_ref, sums) = refs[:nz], refs[nz:]
    z = lax.axis_index("z")
    n = 2 * zf
    for k in range(nz):
        gu = jnp.dot(chunks[k][:n, :], own_ref[0], preferred_element_type=F32)
        gu += jnp.dot(got_ref[k, :n, :], oth_ref[0], preferred_element_type=F32)
        dn = jnp.dot(chunks[k][n : n + zf, :], own_ref[1], preferred_element_type=F32)
        dn += jnp.dot(got_ref[k, n:, :], oth_ref[1], preferred_element_type=F32)
        at = lax.rem(z + order[k], nz)
        sums[at, :n, :] = gu.astype(BF16)
        sums[at, n:, :] = dn.astype(BF16)
    for i in range(0, nz, 2):
        at = pl.ds(i * zf, 2 * zf)
        gate_ref[:, at] = jnp.concatenate([sums[i, :zf, :], sums[i + 1, :zf, :]], axis=0).T
        up_ref[:, at] = jnp.concatenate([sums[i, zf:n, :], sums[i + 1, zf:n, :]], axis=0).T
        down_ref[at, :] = jnp.concatenate([sums[i, n:, :], sums[i + 1, n:, :]], axis=0)


def weight_grads(chunks, order, got, tokens, zf):
    nz, width = len(chunks), tokens[0].shape[2]
    return pl.pallas_call(
        functools.partial(grads_kernel, order, zf),
        out_shape=[
            jax.ShapeDtypeStruct((width, nz * zf), BF16),
            jax.ShapeDtypeStruct((width, nz * zf), BF16),
            jax.ShapeDtypeStruct((nz * zf, width), BF16),
        ],
        scratch_shapes=[pltpu.VMEM((nz, 3 * zf, width), BF16)],
        compiler_params=pltpu.CompilerParams(vmem_limit_bytes=16 * 2**20),
    )(*chunks, got, *tokens)


def per_device(nz, ny, x, wg, wu, wd, c):
    rows, width = x.shape
    fwidth = wg.shape[1]
    zf = fwidth // nz
    z = lax.axis_index("z")
    right = [(i, (i + 1) % nz) for i in range(nz)]
    left = [(i, (i - 1) % nz) for i in range(nz)]

    pair = jnp.concatenate([x, c], axis=1)
    pair = jnp.broadcast_to(pair[None], (ny,) + pair.shape)
    pair = lax.all_to_all(pair, "y", 0, 0, tiled=True).reshape(ny * rows, 2 * width)
    other = swap(pair, "xh")
    part_tokens = pair.shape[0]
    x0, c0 = pair[:, :width], pair[:, width:]
    half = 2 * part_tokens

    gu_own, d_own = in_order(nz, wg, wu, wd)
    gu_oth, d_oth = in_order(nz, swap(wg, "core"), swap(wu, "core"), swap(wd, "core"))
    far = nz // 2

    def part_far(t, u):
        halves = [(gu_own, t), (d_own, u), (gu_oth, t), (d_oth, u)]
        return jnp.concatenate([dot(w[far], v, 1, 1) for w, v in halves], axis=0) * SCALE

    def products(t, u):
        pairs = ((gu_own, t), (d_own, u), (gu_oth, t), (d_oth, u))
        return [(dot(w.reshape(-1, width), v, 1, 1) * SCALE).reshape(nz, -1, part_tokens) for w, v in pairs]

    first = products(x0, c0)
    other, *first = tie(other, *first)
    x1, c1 = other[:, :width], other[:, width:]
    xs, cs = jnp.concatenate([x0, x1], axis=0), jnp.concatenate([c0, c1], axis=0)
    parts = list(zip(first, products(x1, c1)))

    def half_part(i, k):
        return jnp.concatenate([p[i][k] for p in parts], axis=0)

    def part(k):
        return jnp.concatenate([half_part(0, k), half_part(1, k)], axis=1)

    r = lax.ppermute(part_far(x0, c0).astype(F16), "z", right).astype(F32)
    l = lax.ppermute(half_part(1, far).astype(F16), "z", left).astype(F32)
    r = jnp.pad(r, ((0, 0), (0, part_tokens)))
    l = jnp.pad(l, ((0, 0), (part_tokens, 0)))
    for k in range(far - 1, 0, -1):
        r = lax.ppermute((part(k) + r).astype(F16), "z", right).astype(F32)
        l = lax.ppermute((part(nz - k) + l).astype(F16), "z", left).astype(F32)
    total = part(0) + r + l
    got = swap(total.astype(F16), "xl")
    tokens_own = jnp.stack([xs, cs])
    tokens_oth = swap(tokens_own, "core")
    got, tokens_oth = tie(got, tokens_oth)
    total = ((total + got.astype(F32)) * (1.0 / SCALE)).reshape(2, 3, zf, half)
    gate, upper, hidden_grad = total[:, 0], total[:, 1], total[:, 2]

    sig = jax.nn.sigmoid(gate)
    hidden = (gate * sig * upper).astype(BF16)
    gate_delta = (hidden_grad * upper * sig * (1.0 + gate * (1.0 - sig))).astype(BF16)
    up_delta = (hidden_grad * gate * sig).astype(BF16)

    chunk = [None] * nz
    chunk[0] = jnp.stack([gate_delta, up_delta, hidden], axis=1).reshape(6 * zf, half)
    for k in range(1, far):
        chunk[nz - k] = lax.ppermute(chunk[(nz - k + 1) % nz], "z", right)
        chunk[k] = lax.ppermute(chunk[k - 1], "z", left)
    chunk[far] = jnp.concatenate(
        [
            lax.ppermute(chunk[far + 1][:, :part_tokens], "z", right),
            lax.ppermute(chunk[far - 1][:, part_tokens:], "z", left),
        ],
        axis=1,
    )

    order = [0] + [j for i in range(1, far) for j in (nz - i, i)] + [far]
    deltas = jnp.stack([chunk[k][3 * zf :] for k in order[:-1]])
    chunk[far], deltas = tie(chunk[far], deltas)
    send = input_grads(chunk, gu_own, gu_oth, part_tokens, part_tokens, BF16)
    send, *chunk = tie(send, *chunk)
    got = swap(send, "xh")
    total = input_grads(chunk, gu_own, gu_oth, 0, part_tokens, F32)
    deltas = jnp.concatenate([deltas, chunk[far][None, 3 * zf :]], axis=0)
    got, total, deltas = tie(got, total, deltas)
    deltas = swap(deltas, "core")
    total = (total + got.astype(F32)).astype(BF16).reshape(ny, rows, width)
    recv = lax.all_to_all(total, "y", 0, 0, tiled=True)
    tokens = (tokens_own, tokens_oth)
    gate_grad, up_grad, down_grad = weight_grads([chunk[k] for k in order], order, deltas, tokens, zf)
    recv, gate_grad, up_grad, down_grad = tie(recv, gate_grad, up_grad, down_grad)
    input_grad = recv.astype(F32).sum(0).astype(BF16)
    return (input_grad, gate_grad, up_grad, down_grad)


def solution(mesh):
    nz, ny = mesh.shape["gx"] // 2, mesh.shape["gy"] // 4
    grid = Mesh(mesh.devices.reshape(nz, 2, ny, 2, 2), AXES)
    in_specs = (P(GY, GX), P(GX, GY), P(GX, GY), P(GY, GX), P(GY, GX))
    out_specs = (P(GY, GX), P(GX, GY), P(GX, GY), P(GY, GX))
    return jax.shard_map(
        lambda *args: per_device(nz, ny, *args),
        mesh=grid,
        in_specs=in_specs,
        out_specs=out_specs,
        check_vma=False,
    )
```

```python
import functools

import jax
import jax.numpy as jnp
from jax import lax
from jax.experimental import pallas as pl
from jax.experimental.pallas import tpu as pltpu
from jax.sharding import Mesh
from jax.sharding import PartitionSpec as P

AXES = ("z", "xl", "y", "xh", "core")
GX, GY = ("z", "xl"), ("y", "xh", "core")
SCALE = 16.0
F32, BF16, F16 = jnp.float32, jnp.bfloat16, jnp.float16


def dot(a, b, ca, cb):
    return lax.dot_general(a, b, (((ca,), (cb,)), ((), ())), preferred_element_type=F32)


def swap(x, axis):
    return lax.ppermute(x, axis, [(0, 1), (1, 0)])


def tie(*arrays):
    return lax.optimization_barrier(arrays)


def order_kernel(nz, g_ref, u_ref, d_ref, gu_out, d_out):
    z = lax.axis_index("z")
    n = d_ref.shape[0] // nz
    gate, up = g_ref[...].T, u_ref[...].T
    for i in range(nz):
        k = lax.rem(i + nz - z, nz)
        gu_out[k, :n, :] = gate[i * n : (i + 1) * n]
        gu_out[k, n:, :] = up[i * n : (i + 1) * n]
        d_out[k, :, :] = d_ref[i * n : (i + 1) * n, :]


def in_order(nz, wg, wu, wd):
    n, width = wd.shape[0] // nz, wd.shape[1]
    return pl.pallas_call(
        functools.partial(order_kernel, nz),
        out_shape=[
            jax.ShapeDtypeStruct((nz, 2 * n, width), wd.dtype),
            jax.ShapeDtypeStruct((nz, n, width), wd.dtype),
        ],
        compiler_params=pltpu.CompilerParams(vmem_limit_bytes=16 * 2**20),
    )(wg, wu, wd)


def input_kernel(order, at, *refs):
    chunks, (own_ref, oth_ref, out_ref) = refs[: len(refs) - 3], refs[len(refs) - 3 :]
    n, h, step = out_ref.shape[0], own_ref.shape[1], chunks[0].shape[0] // 2
    total = jnp.zeros(out_ref.shape, F32)
    for k, chunk in zip(order, chunks):
        for i, ref in enumerate((own_ref, oth_ref)):
            deltas = chunk[i * step : i * step + h, at : at + n]
            total += lax.dot_general(
                deltas, ref[k], (((0,), (0,)), ((), ())), preferred_element_type=F32
            )
    out_ref[...] = total


def input_grads(chunks, order, own, oth, at, n):
    return pl.pallas_call(
        functools.partial(input_kernel, order, at),
        out_shape=jax.ShapeDtypeStruct((n, own.shape[2]), F32),
        compiler_params=pltpu.CompilerParams(vmem_limit_bytes=16 * 2**20),
    )(*chunks, own, oth)


def grads_kernel(order, zf, *refs):
    nz = len(order)
    chunks, (got_ref, own_ref, oth_ref, gate_ref, up_ref, down_ref, sums) = refs[:nz], refs[nz:]
    z = lax.axis_index("z")
    n = 2 * zf
    for k in range(nz):
        gu = jnp.dot(chunks[k][:n, :], own_ref[0], preferred_element_type=F32)
        gu += jnp.dot(got_ref[k, :n, :], oth_ref[0], preferred_element_type=F32)
        dn = jnp.dot(chunks[k][n : n + zf, :], own_ref[1], preferred_element_type=F32)
        dn += jnp.dot(got_ref[k, n:, :], oth_ref[1], preferred_element_type=F32)
        at = lax.rem(z + order[k], nz)
        sums[at, :n, :] = gu.astype(BF16)
        sums[at, n:, :] = dn.astype(BF16)
    for i in range(0, nz, 2):
        at = pl.ds(i * zf, 2 * zf)
        gate_ref[:, at] = jnp.concatenate([sums[i, :zf, :], sums[i + 1, :zf, :]], axis=0).T
        up_ref[:, at] = jnp.concatenate([sums[i, zf:n, :], sums[i + 1, zf:n, :]], axis=0).T
        down_ref[at, :] = jnp.concatenate([sums[i, n:, :], sums[i + 1, n:, :]], axis=0)


def weight_grads(chunks, order, got, tokens, zf):
    nz, width = len(chunks), tokens[0].shape[2]
    return pl.pallas_call(
        functools.partial(grads_kernel, order, zf),
        out_shape=[
            jax.ShapeDtypeStruct((width, nz * zf), BF16),
            jax.ShapeDtypeStruct((width, nz * zf), BF16),
            jax.ShapeDtypeStruct((nz * zf, width), BF16),
        ],
        scratch_shapes=[pltpu.VMEM((nz, 3 * zf, width), BF16)],
        compiler_params=pltpu.CompilerParams(vmem_limit_bytes=16 * 2**20),
    )(*chunks, got, *tokens)


def per_device(nz, ny, x, wg, wu, wd, c):
    rows, width = x.shape
    fwidth = wg.shape[1]
    zf = fwidth // nz
    z = lax.axis_index("z")
    right = [(i, (i + 1) % nz) for i in range(nz)]
    left = [(i, (i - 1) % nz) for i in range(nz)]

    pair = jnp.concatenate([x, c], axis=1)
    pair = jnp.broadcast_to(pair[None], (ny,) + pair.shape)
    pair = lax.all_to_all(pair, "y", 0, 0, tiled=True).reshape(ny * rows, 2 * width)
    other = swap(pair, "xh")
    part_tokens = pair.shape[0]
    x0, c0 = pair[:, :width], pair[:, width:]
    half = 2 * part_tokens

    gu_own, d_own = in_order(nz, wg, wu, wd)
    gu_oth, d_oth = in_order(nz, swap(wg, "core"), swap(wu, "core"), swap(wd, "core"))
    far = nz // 2

    def part_far(t, u):
        halves = [(gu_own, t), (d_own, u), (gu_oth, t), (d_oth, u)]
        return jnp.concatenate([dot(w[far], v, 1, 1) for w, v in halves], axis=0) * SCALE

    def products(t, u):
        pairs = ((gu_own, t), (d_own, u), (gu_oth, t), (d_oth, u))
        return [(dot(w.reshape(-1, width), v, 1, 1) * SCALE).reshape(nz, -1, part_tokens) for w, v in pairs]

    first = products(x0, c0)
    other, *first = tie(other, *first)
    x1, c1 = other[:, :width], other[:, width:]
    xs, cs = jnp.concatenate([x0, x1], axis=0), jnp.concatenate([c0, c1], axis=0)
    parts = list(zip(first, products(x1, c1)))

    def half_part(i, k):
        return jnp.concatenate([p[i][k] for p in parts], axis=0)

    def part(k):
        return jnp.concatenate([half_part(0, k), half_part(1, k)], axis=1)

    r = lax.ppermute(part_far(x0, c0).astype(F16), "z", right).astype(F32)
    l = lax.ppermute(half_part(1, far).astype(F16), "z", left).astype(F32)
    r = jnp.pad(r, ((0, 0), (0, part_tokens)))
    l = jnp.pad(l, ((0, 0), (part_tokens, 0)))
    for k in range(far - 1, 0, -1):
        r = lax.ppermute((part(k) + r).astype(F16), "z", right).astype(F32)
        l = lax.ppermute((part(nz - k) + l).astype(F16), "z", left).astype(F32)
    total = part(0) + r + l
    got = swap(total.astype(F16), "xl")
    tokens_own = jnp.stack([xs, cs])
    tokens_oth = swap(tokens_own, "core")
    got, tokens_oth = tie(got, tokens_oth)
    total = ((total + got.astype(F32)) * (1.0 / SCALE)).reshape(2, 3, zf, half)
    gate, upper, hidden_grad = total[:, 0], total[:, 1], total[:, 2]

    sig = jax.nn.sigmoid(gate)
    hidden = (gate * sig * upper).astype(BF16)
    gate_delta = (hidden_grad * upper * sig * (1.0 + gate * (1.0 - sig))).astype(BF16)
    up_delta = (hidden_grad * gate * sig).astype(BF16)

    chunk = [None] * nz
    chunk[0] = jnp.stack([gate_delta, up_delta, hidden], axis=1).reshape(6 * zf, half)
    for k in range(1, far):
        chunk[nz - k] = lax.ppermute(chunk[(nz - k + 1) % nz], "z", right)
        chunk[k] = lax.ppermute(chunk[k - 1], "z", left)
    chunk[far] = jnp.concatenate(
        [
            lax.ppermute(chunk[far + 1][:, :part_tokens], "z", right),
            lax.ppermute(chunk[far - 1][:, part_tokens:], "z", left),
        ],
        axis=1,
    )

    order = [0] + [j for i in range(1, far) for j in (nz - i, i)] + [far]
    deltas = jnp.stack([chunk[k][3 * zf :] for k in order[:-1]])
    send = input_grads([chunk[k] for k in order[:-1]], order, gu_own, gu_oth, part_tokens, part_tokens)
    chunk[far], deltas, send = tie(chunk[far], deltas, send)
    for i, w in enumerate((gu_own, gu_oth)):
        send = send + dot(chunk[far][3 * zf * i : 3 * zf * i + 2 * zf, part_tokens:], w[far], 0, 0)
    send, *chunk = tie(send.astype(BF16), *chunk)
    got = swap(send, "xh")
    total = input_grads([chunk[k] for k in order], order, gu_own, gu_oth, 0, part_tokens)
    deltas = jnp.concatenate([deltas, chunk[far][None, 3 * zf :]], axis=0)
    got, total, deltas = tie(got, total, deltas)
    deltas = swap(deltas, "core")
    total = (total + got.astype(F32)).astype(BF16).reshape(ny, rows, width)
    recv = lax.all_to_all(total, "y", 0, 0, tiled=True)
    tokens = (tokens_own, tokens_oth)
    gate_grad, up_grad, down_grad = weight_grads([chunk[k] for k in order], order, deltas, tokens, zf)
    recv, gate_grad, up_grad, down_grad = tie(recv, gate_grad, up_grad, down_grad)
    input_grad = recv.astype(F32).sum(0).astype(BF16)
    return (input_grad, gate_grad, up_grad, down_grad)


def solution(mesh):
    nz, ny = mesh.shape["gx"] // 2, mesh.shape["gy"] // 4
    grid = Mesh(mesh.devices.reshape(nz, 2, ny, 2, 2), AXES)
    in_specs = (P(GY, GX), P(GX, GY), P(GX, GY), P(GY, GX), P(GY, GX))
    out_specs = (P(GY, GX), P(GX, GY), P(GX, GY), P(GY, GX))
    return jax.shard_map(
        lambda *args: per_device(nz, ny, *args),
        mesh=grid,
        in_specs=in_specs,
        out_specs=out_specs,
        check_vma=False,
    )
```
